32 devices in a mesh: parts: 2 (over y), ep: 4 (over z), dp: 2 (over x), tp: 2 (over core).
Axes of the slice: x: 2, y: 2, z: 4, core: 2. Of those that a mesh axis runs over, the one named last changes fastest.
Arguments:
- latent_in: bfloat16 [2048, 1024], P(('parts', 'ep', 'dp')), parts along dimension 0, may hold values from -6 to 6
- out_grad: bfloat16 [2048, 1024], P(('parts', 'ep', 'dp')), parts along dimension 0, may hold values from -6 to 6
- expert_ids: int32 [2048, 2], P(('parts', 'ep', 'dp')), parts along dimension 0, may hold values from 0 to 3, all different within a row; in each aligned block of 128 rows (0 to 127, 128 to 255, ...) at most 72 rows name the same one
- gate_weights: bfloat16 [2048, 2], P(('parts', 'ep', 'dp')), parts along dimension 0, may hold values from 0.049804688 to 0.5
- up_weight: bfloat16 [4, 1024, 1024], P('ep', None, 'tp'), may hold values from -0.1875 to 0.1875
- down_weight: bfloat16 [4, 1024, 1024], P('ep', 'tp'), may hold values from -0.1875 to 0.1875
Outputs:
- latent_out: bfloat16 [2048, 1024], P(('parts', 'ep', 'dp'), 'tp'), parts along dimension 0
- latent_grad: bfloat16 [2048, 1024], P(('parts', 'ep', 'dp'), 'tp'), parts along dimension 0
- grad_up: float32 [8, 1024, 1024], P(('parts', 'ep'), 'dp', 'tp'), parts along dimension 0
- grad_down: float32 [8, 1024, 1024], P(('parts', 'ep'), 'tp', 'dp'), parts along dimension 0
The draws below stay inside these ranges and needn't reach their ends.
There are 2 independent parts, one for each index of `parts`. The reference program is written for one: setup_inputs(seed, part) draws one part's arguments, and reference() takes and returns one part's arrays. A program takes and returns all parts, laid end to end along the dimension named above; an argument that names none is the same for every part. Nothing has to cross between parts.
Inputs may be any that keep to these rules, and one draw needn't show every extreme that they name: `expert_ids`: each row names 2 different experts. In the 128 rows of one device no expert is named more than 72 times, a bound that some block reaches.
All inputs are finite; a program needn't handle non-finite values.
Results may differ from the reference program's by a relative error of at most 0.011.
Values may be sent and summed in bfloat16 or wider, within the bound.
A program may use at most 64 MiB of HBM per device.

```python
import math
import jax
import jax.numpy as jnp
import numpy as np
from jax import lax

L = 1024
F = 1024
TOK_DEV = 128
EXPERTS = 4
TOP = 2
CAP = 72
TOKENS = 1024
N_EP = 4
N_DP = 2
N_TP = 2


def raised(array, rng, source, target, blocks, factor):
    def block_of(axis_at):
        return (jnp.arange(array.shape[axis_at]) // (array.shape[axis_at] // blocks)).reshape((-1,) + (1,) * (array.ndim - 1 - axis_at))

    one_side = jax.random.permutation(rng, blocks)[block_of(target)]
    second = (block_of(target) + blocks // 2) % blocks
    return jnp.where((block_of(source) == one_side) | (block_of(source) == second), factor * array, array)


def shard_levels(rng, shape, split, smallest, top_value):
    def one(axis_at, shards_of):
        draws = jax.random.uniform(jax.random.fold_in(jax.random.fold_in(rng, 6), axis_at), (shards_of,), jnp.float32, smallest / len(split), top_value / len(split))
        return jnp.repeat(jnp.exp(draws), shape[axis_at] // shards_of).reshape((-1,) + (1,) * (len(shape) - axis_at - 1))

    gain = one(*split[0])
    for cut in split[1:]:
        gain = gain * one(*cut)
    return gain


def routed_block(key, own, number, rows, number_of, top, bound, skew):
    ranking = jax.random.permutation(key, number_of)
    crowded, usual = portions_of(number_of, rows * top, bound, skew, True), portions_of(number_of, rows * top, bound, skew, False)
    places = jnp.arange(number_of)

    def named(lengths, turn):
        used = int((lengths > 0).sum())
        fixed = max(1, used // 4)
        moved = fixed + (places - fixed + turn * (used - fixed)) % max(1, number_of - fixed)
        return jnp.zeros((number_of,), jnp.int32).at[ranking[jnp.where(places < fixed, places, moved)]].set(jnp.asarray(lengths, jnp.int32))

    lengths = jnp.where(number % 4 == 0, named(crowded, number // 4), named(usual, number - number // 4 - 1))
    mixed = jax.random.permutation(jax.random.fold_in(own, 3), number_of)
    donor, sink = mixed[0:number_of // 2 * 2:2], mixed[1:number_of // 2 * 2:2]
    margin = jnp.minimum(lengths[donor] - 1, bound - lengths[sink]) // 2
    margin = jnp.where((donor == ranking[0]) | (sink == ranking[0]) | (lengths[sink] == 0), 0, jnp.maximum(margin, 0))
    moved = jax.random.randint(jax.random.fold_in(own, 4), (number_of // 2,), 0, 1 << 20) % (margin + 1)
    lengths = lengths.at[donor].add(-moved).at[sink].add(moved)
    members = jnp.searchsorted(jnp.cumsum(lengths), jnp.arange(rows * top), side="right").astype(jnp.int32)
    table = members.reshape(top, rows).T
    table = table[jax.random.permutation(jax.random.fold_in(own, 1), rows)]
    turn = jax.random.randint(jax.random.fold_in(own, 2), (rows, 1), 0, top)
    return jnp.take_along_axis(table, (jnp.arange(top)[None, :] + turn) % top, axis=1)


def portions_of(amount, total, bound, slope, full):
    weights = [(1 << 20) // math.isqrt(standing ** slope) + 1 for standing in range(1, amount + 1)]
    largest = bound if full else min(bound, max(-(-total // amount), total * weights[0] // sum(weights)))
    least = 1 if total - largest >= amount - 1 else 0
    counts, spare = [largest] + [least] * (amount - 1), total - largest - least * (amount - 1)
    while spare > 0:
        candidates = [i for i in range(1, amount) if counts[i] < largest] or [i for i in range(1, amount) if counts[i] < bound]
        mass, left = sum([weights[i] for i in candidates]), spare
        for i in candidates:
            addition = min(bound - counts[i], max(1, left * weights[i] // mass), spare)
            counts[i] = counts[i] + addition
            spare = spare - addition
    return np.array(counts)


def gaussian(rng, dims, deviation, bound, split=(), kind=jnp.bfloat16):
    drawn = deviation * jax.random.normal(rng, dims, jnp.float32)
    if split:
        drawn = drawn * shard_levels(rng, dims, split, -0.22, 0.18)
    return jnp.clip(drawn, -bound, bound).astype(kind)


def bell_draw_with(rng, shape, deviation, most, pieces, heavy, kind=jnp.bfloat16):
    array = deviation * jax.random.normal(rng, shape, jnp.float32)
    if pieces:
        array = array * shard_levels(rng, shape, pieces, -0.22, 0.18)
    return jnp.clip(raised(array, jax.random.fold_in(rng, 3), *heavy), -most, most).astype(kind)


def setup_inputs(seed: int = 0, part: int = 0) -> dict:
    keys = jax.random.split(jax.random.key(seed), 7)
    part_splits = jax.random.split(jax.random.fold_in(keys[6], part), 7)
    latent_in = gaussian(part_splits[0], (TOKENS, L), 1.0, 6.0, ((0, 8),))
    out_grad = bell_draw_with(part_splits[1], (TOKENS, L), 1.0, 6.0, ((0, 8),), (0, 1, 8, 2.0))
    expert_ids_keys = jax.random.split(jax.random.fold_in(part_splits[2], 1), TOKENS // TOK_DEV)
    expert_ids_turns = jax.random.permutation(jax.random.fold_in(part_splits[2], 3), TOKENS // TOK_DEV)
    expert_ids = jax.vmap(lambda own, number: routed_block(jax.random.fold_in(part_splits[2], 2), own, number, TOK_DEV, EXPERTS, TOP, CAP, 2))(expert_ids_keys, expert_ids_turns).reshape((TOKENS, TOP))
    gate_weights = jnp.clip(jnp.exp(math.log(0.5) - 2.306499 * jax.random.uniform(part_splits[3], (TOKENS, TOP), jnp.float32) ** shard_levels(part_splits[3], (TOKENS, TOP), ((0, 8),), -0.2, 0.2)), 0.049804688, 0.5).astype(jnp.bfloat16)
    up_weight = gaussian(keys[4], (EXPERTS, L, F), L ** -0.5, 0.1875, ((0, 4), (2, 2)))
    down_weight = gaussian(keys[5], (EXPERTS, F, L), F ** -0.5, 0.1875, ((0, 4), (1, 2)))
    return {"latent_in": latent_in, "out_grad": out_grad, "expert_ids": expert_ids, "gate_weights": gate_weights, "up_weight": up_weight, "down_weight": down_weight}


def regroup_rows(values):
    shaped = values.reshape(N_EP, N_DP, CAP, values.shape[-1]).astype(jnp.float32)
    return jnp.transpose(shaped, (1, 0, 2, 3)).reshape(N_DP, N_EP * CAP, values.shape[-1])


def replica_sum(left_operand, right_operand):
    running_sum_parts = jnp.einsum("qyo,qyn->qon", regroup_rows(left_operand), regroup_rows(right_operand))
    rounded = lax.optimization_barrier(running_sum_parts.astype(jnp.bfloat16))
    return jnp.sum(rounded.astype(jnp.float32), axis=0)


def reference(latent_in, out_grad, expert_ids, gate_weights, up_weight, down_weight):
    block_count = N_EP * N_DP
    pair_count = TOK_DEV * TOP
    row_count = block_count * CAP
    half_hidden = F // N_TP
    routed = expert_ids.reshape(block_count, pair_count)
    onehot = (routed[:, :, None] == jnp.arange(EXPERTS, dtype=jnp.int32)[None, None, :]).astype(jnp.int32)
    position = jnp.sum(jnp.cumsum(onehot, axis=1) * onehot, axis=2).astype(jnp.int32) - 1
    block_index = jnp.broadcast_to(jnp.arange(block_count, dtype=jnp.int32)[:, None], (block_count, pair_count))
    token_position = block_index * TOK_DEV + (jnp.arange(pair_count, dtype=jnp.int32) // TOP)[None, :]
    source = jnp.full((EXPERTS, block_count, CAP), TOKENS, jnp.int32).at[routed, block_index, position].set(token_position)
    scales = jnp.zeros((EXPERTS, block_count, CAP), jnp.bfloat16).at[routed, block_index, position].set(
        gate_weights.reshape(block_count, pair_count))
    zero_row = jnp.zeros((1, L), jnp.bfloat16)
    padded_in = jnp.concatenate([latent_in, zero_row], axis=0)
    padded_grad = jnp.concatenate([out_grad, zero_row], axis=0)

    def expert(totals, inputs):
        out_total, in_total = totals
        source_e, scale_e, expert_up, expert_down = inputs
        flat_source = source_e.reshape(row_count)
        flat_scale = scale_e.reshape(row_count, 1).astype(jnp.float32)
        gathered = padded_in[flat_source]
        scaled = (flat_scale * padded_grad[flat_source].astype(jnp.float32)).astype(jnp.bfloat16)
        preact = jnp.dot(gathered, expert_up, preferred_element_type=jnp.float32)
        positive = jnp.maximum(preact, 0.0)
        hidden_state = (positive * positive).astype(jnp.bfloat16)
        down_split = expert_down.reshape(N_TP, half_hidden, L).astype(jnp.float32)
        output_part = jnp.einsum("rjf,jfl->rjl", hidden_state.reshape(row_count, N_TP, half_hidden).astype(jnp.float32),
                                 down_split).astype(jnp.bfloat16)
        hidden_grad = jnp.dot(scaled, expert_down.T, preferred_element_type=jnp.float32)
        preact_grad = (2.0 * hidden_grad * positive).astype(jnp.bfloat16)
        up_split = expert_up.reshape(L, N_TP, half_hidden).astype(jnp.float32)
        input_part = jnp.einsum("rjf,ljf->rjl", preact_grad.reshape(row_count, N_TP, half_hidden).astype(jnp.float32),
                                up_split).astype(jnp.bfloat16)
        output_rows = jnp.sum(output_part.astype(jnp.float32), axis=1) * flat_scale
        input_rows = jnp.sum(input_part.astype(jnp.float32), axis=1)
        out_total = out_total.at[flat_source].add(output_rows)
        in_total = in_total.at[flat_source].add(input_rows)
        up_grad = replica_sum(gathered, preact_grad)
        down_grad = replica_sum(hidden_state, scaled)
        return (out_total, in_total), (up_grad, down_grad)

    start = (jnp.zeros((TOKENS + 1, L), jnp.float32), jnp.zeros((TOKENS + 1, L), jnp.float32))
    totals, stacked = lax.scan(expert, start, (source, scales, up_weight, down_weight))
    out_total, in_total = totals
    grad_up, grad_down = stacked
    return (out_total[:TOKENS].astype(jnp.bfloat16), in_total[:TOKENS].astype(jnp.bfloat16), grad_up, grad_down)
```

```python
import functools

import jax
import jax.numpy as jnp
from jax import lax
from jax.experimental import pallas as pl
from jax.experimental.pallas import tpu as pltpu
from jax.sharding import PartitionSpec as P

MESH = pl.DeviceIdType.MESH
NT = (((1,), (1,)), ((), ()))
TN = (((0,), (0,)), ((), ()))


def dot(a, b, dims=(((1,), (0,)), ((), ()))):
    return lax.dot_general(a, b, dims, preferred_element_type=jnp.float32)


def kernel(
    n_ep, n_dp, cap,
    x_ref, g_ref, ids_ref, gate_ref, up_hbm, down_hbm,
    out_ref, in_ref, gu_ref, gd_ref,
    up, down, disp, other, recv, b_up, b_dn, part, got, mine, ret, back, gu, gd, route,
    w_sem, z_send, z_recv, s_send, s_recv, x_send, x_recv, p_send, p_recv, r_send, r_recv, o_sem,
):
    z, d, c = lax.axis_index("ep"), lax.axis_index("dp"), lax.axis_index("tp")
    sib = 1 - c
    rows = 2 * cap
    tok, width = x_ref.shape
    half = width // 2
    fanout = ids_ref.shape[1]
    bf = jnp.bfloat16

    def peer(i):
        if n_ep == 4 and isinstance(i, int):
            return (z, z + 1 - 2 * lax.rem(z, 2), lax.rem(z + 2, 4), 3 - z)[i]
        return lax.rem(z + i, n_ep)

    def each(order, body):
        if n_ep == 4:
            for i in order:
                body(i)
        else:
            lax.fori_loop(1, n_ep, lambda i, _: (body(i), 0)[1], 0)

    barrier = pltpu.get_barrier_semaphore()

    def greet(i, _):
        pl.semaphore_signal(
            barrier, inc=1, device_id={"ep": lax.rem(z + i, n_ep)}, device_id_type=MESH)
        return 0

    lax.fori_loop(1, n_ep, greet, 0)
    for j in range(1, n_dp):
        pl.semaphore_signal(
            barrier, inc=1, device_id={"dp": lax.rem(d + j, n_dp)}, device_id_type=MESH)
    pl.semaphore_signal(barrier, inc=1, device_id={"tp": sib}, device_id_type=MESH)

    load_up = pltpu.make_async_copy(up_hbm.at[0], up, w_sem.at[0])
    load_down = pltpu.make_async_copy(down_hbm.at[0], down, w_sem.at[1])
    load_up.start()
    load_down.start()

    ids = ids_ref[...]
    lanes = lax.broadcasted_iota(jnp.int32, (tok, 128), 1)
    picks = [(lanes == ids[:, k:k + 1]).astype(jnp.float32) for k in range(fanout)]
    named = functools.reduce(lambda a, b: a + b, picks).astype(bf)
    earlier = (
        lax.broadcasted_iota(jnp.int32, (tok, tok), 1)
        < lax.broadcasted_iota(jnp.int32, (tok, tok), 0)
    ).astype(jnp.float32).astype(bf)
    before = dot(earlier, named)
    slots = lax.broadcasted_iota(jnp.int32, (tok, n_ep * rows), 1).astype(jnp.float32)
    zero = jnp.zeros(slots.shape, jnp.float32)
    first, second, first_w, second_w = zero, zero, zero, zero
    for k in range(fanout):
        place = jnp.sum(picks[k] * before, axis=1, keepdims=True)
        target = ids[:, k:k + 1].astype(jnp.float32) * float(rows) + place
        weight = gate_ref[:, k:k + 1].astype(jnp.float32)
        hit, hit2 = slots == target, slots == target + float(cap)
        first = first + jnp.where(hit, 1.0, 0.0)
        first_w = first_w + jnp.where(hit, weight, 0.0)
        second = second + jnp.where(hit2, 1.0, 0.0)
        second_w = second_w + jnp.where(hit2, weight, 0.0)
    spread = jnp.concatenate([first, second_w], axis=0).astype(bf)
    route[...] = jnp.concatenate([first_w, second], axis=0).astype(bf)

    def sent_columns(h):
        cols = pl.ds(pl.multiple_of(h * half, 128), half)
        source = jnp.concatenate([x_ref[:, cols], g_ref[:, cols]], axis=0)
        return dot(spread, source, TN).astype(bf).reshape(n_ep, rows, half)

    disp[...] = sent_columns(c)
    pl.semaphore_wait(barrier, n_ep - 1 + n_dp - 1 + 1)

    def z_copy(dst, src):
        return pltpu.make_async_remote_copy(
            src_ref=disp.at[dst], dst_ref=recv.at[d, c, src],
            send_sem=z_send.at[dst], recv_sem=z_recv.at[src],
            device_id={"ep": dst}, device_id_type=MESH)

    def z_arrival(src):
        return pltpu.make_async_remote_copy(
            src_ref=disp.at[src], dst_ref=recv.at[d, c, src],
            send_sem=z_send.at[src], recv_sem=z_recv.at[src],
            device_id={"ep": src}, device_id_type=MESH)

    def x_copy(to, src):
        return pltpu.make_async_remote_copy(
            src_ref=recv.at[d, c, src], dst_ref=recv.at[d, c, src],
            send_sem=x_send.at[to, src], recv_sem=x_recv.at[d, src],
            device_id={"dp": to}, device_id_type=MESH)

    def x_arrival(frm, src):
        return pltpu.make_async_remote_copy(
            src_ref=recv.at[frm, c, src], dst_ref=recv.at[frm, c, src],
            send_sem=x_send.at[frm, src], recv_sem=x_recv.at[frm, src],
            device_id={"dp": frm}, device_id_type=MESH)

    def s_copy(group, src):
        return pltpu.make_async_remote_copy(
            src_ref=recv.at[group, c, src], dst_ref=recv.at[group, c, src],
            send_sem=s_send.at[group, src], recv_sem=s_recv.at[group, src],
            device_id={"tp": sib}, device_id_type=MESH)

    def s_arrival(group, src):
        return pltpu.make_async_remote_copy(
            src_ref=recv.at[group, sib, src], dst_ref=recv.at[group, sib, src],
            send_sem=s_send.at[group, src], recv_sem=s_recv.at[group, src],
            device_id={"tp": sib}, device_id_type=MESH)

    def p_copy(src):
        return pltpu.make_async_remote_copy(
            src_ref=part.at[src], dst_ref=got.at[src],
            send_sem=p_send.at[src], recv_sem=p_recv.at[src],
            device_id={"tp": sib}, device_id_type=MESH)

    def r_copy(src):
        return pltpu.make_async_remote_copy(
            src_ref=ret.at[src], dst_ref=back.at[z],
            send_sem=r_send.at[src], recv_sem=r_recv.at[z],
            device_id={"ep": src}, device_id_type=MESH)

    def r_arrival(exp):
        return pltpu.make_async_remote_copy(
            src_ref=ret.at[exp], dst_ref=back.at[exp],
            send_sem=r_send.at[exp], recv_sem=r_recv.at[exp],
            device_id={"ep": exp}, device_id_type=MESH)

    each((2, 3, 1), lambda i: z_copy(peer(i), z).start())

    other[...] = sent_columns(sib)
    recv[d, c, z] = disp[z]
    recv[d, sib, z] = other[z]
    for j in range(1, n_dp):
        x_copy(lax.rem(d + j, n_dp), z).start()
    load_up.wait()
    load_down.wait()

    def expert(group, src):
        left, right = recv[group, 0, src], recv[group, 1, src]
        left, right = left.astype(jnp.float32), right.astype(jnp.float32)
        r0, r1 = left[:cap].astype(bf), right[:cap].astype(bf)
        g0, g1 = left[cap:].astype(bf), right[cap:].astype(bf)
        preact = dot(r0, up[:half, :]) + dot(r1, up[half:, :])
        hidden_grad = dot(g0, down[:, :half], NT) + dot(g1, down[:, half:], NT)
        positive = jnp.maximum(preact, 0.0)
        hidden = positive * positive
        preact_grad = 2.0 * hidden_grad * positive
        nought = jnp.zeros_like(hidden)
        b_up[group, src] = jnp.concatenate([preact_grad, nought], axis=0).astype(bf)
        b_dn[group, src] = jnp.concatenate([nought, hidden], axis=0).astype(bf)
        return hidden.astype(bf), preact_grad.astype(bf)

    def columns_of(hidden, preact_grad, h):
        cols = pl.ds(pl.multiple_of(h * half, 128), half)
        return jnp.concatenate(
            [dot(hidden, down[:, cols]), dot(preact_grad, up[cols, :], NT)], axis=0)

    def first_pass(src):
        hidden, preact_grad = expert(d, src)
        part[src] = columns_of(hidden, preact_grad, sib).astype(bf)
        p_copy(src).start()
        mine[src] = columns_of(hidden, preact_grad, c)

    def finish(src):
        p_copy(src).wait_recv()
        return (mine[src] + got[src].astype(jnp.float32)).astype(bf)

    first_pass(z)

    def block(i):
        src, last = peer(i), peer(i - 1)
        z_arrival(src).wait_recv()
        s_copy(d, src).start()
        for j in range(1, n_dp):
            x_copy(lax.rem(d + j, n_dp), src).start()
        if isinstance(i, int):
            if i == 1:
                back[z] = finish(z)
            else:
                ret[last] = finish(last)
                r_copy(last).start()
        else:
            ret[last] = finish(last)

            @pl.when(i == 1)
            def _():
                back[z] = ret[z]

            @pl.when(i > 1)
            def _():
                r_copy(last).start()
        s_arrival(d, src).wait_recv()
        first_pass(src)

    each((1, 2, 3), block)
    end = peer(n_ep - 1)
    ret[end] = finish(end)
    r_copy(end).start()

    def pass_on(t, _):
        frm, src = lax.rem(d + 1 + t // n_ep, n_dp), lax.rem(z + t, n_ep)
        x_arrival(frm, src).wait_recv()
        s_copy(frm, src).start()
        return 0

    lax.fori_loop(0, (n_dp - 1) * n_ep, pass_on, 0)

    def replica(t, _):
        frm, src = lax.rem(d + 1 + t // n_ep, n_dp), lax.rem(z + t, n_ep)
        s_arrival(frm, src).wait_recv()
        expert(frm, src)
        return 0

    lax.fori_loop(0, (n_dp - 1) * n_ep, replica, 0)

    share = width // n_dp
    at = d * share

    def gradients(group, _):
        if share == half:
            held = recv[group, d]
        else:
            held = recv[group, at // half, :, :, pl.ds(
                pl.multiple_of(lax.rem(at, half), 128), share)]
        held = held.reshape(n_ep * rows, share)
        inner = b_up.shape[-1]
        gu[group] = dot(held, b_up[group].reshape(n_ep * rows, inner), TN).astype(bf)
        gd[group] = dot(b_dn[group].reshape(n_ep * rows, inner), held, TN).astype(bf)
        return 0

    lax.fori_loop(0, n_dp, gradients, 0)
    store_up = pltpu.make_async_copy(gu, gu_ref, o_sem.at[0])
    store_down = pltpu.make_async_copy(gd, gd_ref, o_sem.at[1])
    store_up.start()
    store_down.start()

    each((1, 2, 3), lambda i: r_arrival(peer(i)).wait_recv())
    total = dot(route[...], back[...].reshape(n_ep * rows, half))
    out_ref[...] = total[:tok].astype(bf)
    in_ref[...] = total[tok:].astype(bf)

    def drain(i):
        z_copy(peer(i), z).wait_send()
        s_copy(d, peer(i)).wait_send()
        r_copy(peer(i)).wait_send()

    each((1, 2, 3), drain)

    def drain_all(t, _):
        p_copy(t).wait_send()
        for j in range(1, n_dp):
            x_copy(lax.rem(d + j, n_dp), t).wait_send()
            s_copy(lax.rem(d + j, n_dp), t).wait_send()
        return 0

    lax.fori_loop(0, n_ep, drain_all, 0)
    store_up.wait()
    store_down.wait()


def body(mesh, latent_in, out_grad, expert_ids, gate_weights, up_weight, down_weight):
    n_ep, n_dp = mesh.shape["ep"], mesh.shape["dp"]
    tok, width = latent_in.shape
    inner = up_weight.shape[2]
    assert up_weight.shape[0] == 1 and mesh.shape["tp"] == 2
    cap = 9 * tok * expert_ids.shape[1] // (8 * n_ep)
    cap = -(-cap // 8) * 8
    rows, half, share = 2 * cap, width // 2, width // n_dp
    bf, f32 = jnp.bfloat16, jnp.float32
    vmem, anyw = pl.BlockSpec(memory_space=pltpu.VMEM), pl.BlockSpec(memory_space=pl.ANY)
    dma = pltpu.SemaphoreType.DMA
    block = (n_ep, rows, half)
    out, lin, gu, gd = pl.pallas_call(
        functools.partial(kernel, n_ep, n_dp, cap),
        out_shape=(
            jax.ShapeDtypeStruct((tok, half), bf),
            jax.ShapeDtypeStruct((tok, half), bf),
            jax.ShapeDtypeStruct((n_dp, share, inner), bf),
            jax.ShapeDtypeStruct((n_dp, inner, share), bf),
        ),
        in_specs=[vmem, vmem, vmem, vmem, anyw, anyw],
        out_specs=(vmem, vmem, anyw, anyw),
        scratch_shapes=[
            pltpu.VMEM((width, inner), bf),
            pltpu.VMEM((inner, width), bf),
            pltpu.VMEM(block, bf),
            pltpu.VMEM(block, bf),
            pltpu.VMEM((n_dp, 2) + block, bf),
            pltpu.VMEM((n_dp, n_ep, rows, inner), bf),
            pltpu.VMEM((n_dp, n_ep, rows, inner), bf),
            pltpu.VMEM(block, bf),
            pltpu.VMEM(block, bf),
            pltpu.VMEM(block, f32),
            pltpu.VMEM(block, bf),
            pltpu.VMEM(block, bf),
            pltpu.VMEM((n_dp, share, inner), bf),
            pltpu.VMEM((n_dp, inner, share), bf),
            pltpu.VMEM((2 * tok, n_ep * rows), bf),
            dma((2,)), dma((n_ep,)), dma((n_ep,)), dma((n_dp, n_ep)), dma((n_dp, n_ep)),
            dma((n_dp, n_ep)), dma((n_dp, n_ep)), dma((n_ep,)), dma((n_ep,)),
            dma((n_ep,)), dma((n_ep,)), dma((2,)),
        ],
        compiler_params=pltpu.CompilerParams(
            collective_id=0, has_side_effects=True, vmem_limit_bytes=48 * 1024 * 1024),
        name="routed_experts",
    )(latent_in, out_grad, expert_ids, gate_weights, up_weight, down_weight)
    grad_up = functools.reduce(lambda a, b: a + b, [gu[i].astype(f32) for i in range(n_dp)])
    grad_down = functools.reduce(lambda a, b: a + b, [gd[i].astype(f32) for i in range(n_dp)])
    return out, lin, grad_up[None], grad_down[None]


def solution(mesh):
    return jax.shard_map(
        functools.partial(body, mesh),
        mesh=mesh,
        in_specs=(
            P(("parts", "ep", "dp"), None),
            P(("parts", "ep", "dp"), None),
            P(("parts", "ep", "dp"), None),
            P(("parts", "ep", "dp"), None),
            P("ep", None, "tp"),
            P("ep", "tp", None),
        ),
        out_specs=(
            P(("parts", "ep", "dp"), "tp"),
            P(("parts", "ep", "dp"), "tp"),
            P(("parts", "ep"), "dp", "tp"),
            P(("parts", "ep"), "tp", "dp"),
        ),
        check_vma=False,
    )
```

```python
import functools

import jax
import jax.numpy as jnp
from jax import lax
from jax.experimental import pallas as pl
from jax.experimental.pallas import tpu as pltpu
from jax.sharding import PartitionSpec as P

MESH = pl.DeviceIdType.MESH
NT = (((1,), (1,)), ((), ()))
TN = (((0,), (0,)), ((), ()))


def dot(a, b, dims=(((1,), (0,)), ((), ()))):
    return lax.dot_general(a, b, dims, preferred_element_type=jnp.float32)


def kernel(
    n_ep, n_dp, cap,
    x_hbm, g_hbm, ids_hbm, gate_hbm, up_hbm, down_hbm,
    gu_ref, gd_ref, out_ref, in_ref,
    x_ref, g_ref, ids_ref, gate_ref, up, down, disp, recv, b_up, b_dn, part, got, mine, ret, back, route, acc, gu, gd,
    w_sem, z_send, z_recv, s_send, s_recv, x_send, x_recv, p_send, p_recv, r_send, r_recv, o_sem,
):
    z, d, c = lax.axis_index("ep"), lax.axis_index("dp"), lax.axis_index("tp")
    sib = 1 - c
    rows = 2 * cap
    tok, width = x_ref.shape
    half = width // 2
    fanout = ids_ref.shape[0]
    bf = jnp.bfloat16

    def peer(i):
        if n_ep == 4 and isinstance(i, int):
            return (z, z + 1 - 2 * lax.rem(z, 2), lax.rem(z + 2, 4), 3 - z)[i]
        return lax.rem(z + i, n_ep)

    def each(order, body):
        if n_ep == 4:
            for i in order:
                body(i)
        else:
            lax.fori_loop(1, n_ep, lambda i, _: (body(i), 0)[1], 0)

    load_x = pltpu.make_async_copy(x_hbm, x_ref, w_sem.at[0])
    load_g = pltpu.make_async_copy(g_hbm, g_ref, w_sem.at[1])
    load_up = pltpu.make_async_copy(up_hbm.at[0], up, w_sem.at[2])
    load_down = pltpu.make_async_copy(down_hbm.at[0], down, w_sem.at[3])
    load_ids = pltpu.make_async_copy(ids_hbm, ids_ref, w_sem.at[4])
    load_gate = pltpu.make_async_copy(gate_hbm, gate_ref, w_sem.at[5])
    load_ids.start()
    load_gate.start()
    load_x.start()
    load_g.start()
    barrier = pltpu.get_barrier_semaphore()

    def greet(i, _):
        pl.semaphore_signal(
            barrier, inc=1, device_id={"ep": lax.rem(z + i, n_ep)}, device_id_type=MESH)
        return 0

    lax.fori_loop(1, n_ep, greet, 0)
    for j in range(1, n_dp):
        pl.semaphore_signal(
            barrier, inc=1, device_id={"dp": lax.rem(d + j, n_dp)}, device_id_type=MESH)
    pl.semaphore_signal(barrier, inc=1, device_id={"tp": sib}, device_id_type=MESH)

    load_up.start()
    load_down.start()

    load_ids.wait()
    load_gate.wait()
    ids = ids_ref[...]
    height = -(-n_ep // 16) * 16
    numbers = lax.broadcasted_iota(jnp.int32, (height, tok), 0)
    picks = [(numbers == ids[k:k + 1, :]).astype(jnp.float32) for k in range(fanout)]
    named = functools.reduce(lambda a, b: a + b, picks).astype(bf)
    earlier = (
        lax.broadcasted_iota(jnp.int32, (tok, tok), 0)
        < lax.broadcasted_iota(jnp.int32, (tok, tok), 1)
    ).astype(jnp.float32).astype(bf)
    before = dot(named, earlier)
    gate = gate_ref[...].astype(jnp.float32)
    targets = [
        ids[k:k + 1, :].astype(jnp.float32) * float(rows)
        + jnp.sum(picks[k] * before, axis=0, keepdims=True)
        for k in range(fanout)]
    row = lax.broadcasted_iota(jnp.int32, (rows, tok), 0)

    def hits(exp, shift, weighted):
        slots = (row + (exp * rows - shift)).astype(jnp.float32)
        found = [
            jnp.where(slots == targets[k], gate[k:k + 1, :] if weighted else 1.0, 0.0)
            for k in range(fanout)]
        return functools.reduce(lambda a, b: a + b, found)

    def columns(h):
        return pl.ds(pl.multiple_of(h * half, 128), half)

    def build(exp, h):
        spread = jnp.concatenate(
            [hits(exp, 0, False), hits(exp, cap, True)], axis=1).astype(bf)
        source = jnp.concatenate([x_ref[:, columns(h)], g_ref[:, columns(h)]], axis=0)
        return dot(spread, source).astype(bf)

    load_x.wait()
    load_g.wait()

    def z_copy(dst, src):
        return pltpu.make_async_remote_copy(
            src_ref=disp.at[dst], dst_ref=recv.at[d, c, src],
            send_sem=z_send.at[dst], recv_sem=z_recv.at[src],
            device_id={"ep": dst}, device_id_type=MESH)

    def z_arrival(src):
        return pltpu.make_async_remote_copy(
            src_ref=disp.at[src], dst_ref=recv.at[d, c, src],
            send_sem=z_send.at[src], recv_sem=z_recv.at[src],
            device_id={"ep": src}, device_id_type=MESH)

    def x_copy(to, src):
        return pltpu.make_async_remote_copy(
            src_ref=recv.at[d, c, src], dst_ref=recv.at[d, c, src],
            send_sem=x_send.at[to, src], recv_sem=x_recv.at[d, src],
            device_id={"dp": to}, device_id_type=MESH)

    def x_arrival(frm, src):
        return pltpu.make_async_remote_copy(
            src_ref=recv.at[frm, c, src], dst_ref=recv.at[frm, c, src],
            send_sem=x_send.at[frm, src], recv_sem=x_recv.at[frm, src],
            device_id={"dp": frm}, device_id_type=MESH)

    def s_copy(group, src):
        return pltpu.make_async_remote_copy(
            src_ref=recv.at[group, c, src], dst_ref=recv.at[group, c, src],
            send_sem=s_send.at[group, src], recv_sem=s_recv.at[group, src],
            device_id={"tp": sib}, device_id_type=MESH)

    def s_arrival(group, src):
        return pltpu.make_async_remote_copy(
            src_ref=recv.at[group, sib, src], dst_ref=recv.at[group, sib, src],
            send_sem=s_send.at[group, src], recv_sem=s_recv.at[group, src],
            device_id={"tp": sib}, device_id_type=MESH)

    def p_copy(src):
        return pltpu.make_async_remote_copy(
            src_ref=part.at[src], dst_ref=got.at[src],
            send_sem=p_send.at[src], recv_sem=p_recv.at[src],
            device_id={"tp": sib}, device_id_type=MESH)

    def r_copy(src):
        return pltpu.make_async_remote_copy(
            src_ref=ret.at[src], dst_ref=back.at[z],
            send_sem=r_send.at[src], recv_sem=r_recv.at[z],
            device_id={"ep": src}, device_id_type=MESH)

    def r_arrival(exp):
        return pltpu.make_async_remote_copy(
            src_ref=ret.at[exp], dst_ref=back.at[exp],
            send_sem=r_send.at[exp], recv_sem=r_recv.at[exp],
            device_id={"ep": exp}, device_id_type=MESH)

    def send(i):
        dst = peer(i)
        disp[dst] = build(dst, c)
        z_copy(dst, z).start()

    if n_ep == 4:
        disp[peer(2)] = build(peer(2), c)
        pl.semaphore_wait(barrier, n_ep + n_dp - 1)
        z_copy(peer(2), z).start()
        send(1)
        disp[peer(3)] = build(peer(3), c)
    else:
        pl.semaphore_wait(barrier, n_ep + n_dp - 1)
        each((), send)

    recv[d, c, z] = build(z, c)
    recv[d, sib, z] = build(z, sib)
    for j in range(1, n_dp):
        x_copy(lax.rem(d + j, n_dp), z).start()

    def weigh(exp, _):
        route[exp] = jnp.concatenate(
            [hits(exp, 0, True), hits(exp, cap, False)], axis=1).astype(bf)
        return 0

    lax.fori_loop(0, n_ep, weigh, 0)
    load_up.wait()
    load_down.wait()

    def expert(group, src):
        left, right = recv[group, 0, src], recv[group, 1, src]
        left, right = left.astype(jnp.float32), right.astype(jnp.float32)
        r0, r1 = left[:cap].astype(bf), right[:cap].astype(bf)
        g0, g1 = left[cap:].astype(bf), right[cap:].astype(bf)
        preact = dot(r0, up[:half, :]) + dot(r1, up[half:, :])
        hidden_grad = dot(g0, down[:, :half], NT) + dot(g1, down[:, half:], NT)
        positive = jnp.maximum(preact, 0.0)
        hidden = positive * positive
        preact_grad = 2.0 * hidden_grad * positive
        nought = jnp.zeros_like(hidden)
        b_up[group, src] = jnp.concatenate([preact_grad, nought], axis=0).astype(bf)
        b_dn[group, src] = jnp.concatenate([nought, hidden], axis=0).astype(bf)
        return hidden.astype(bf), preact_grad.astype(bf)

    def columns_of(hidden, preact_grad, h):
        cols = pl.ds(pl.multiple_of(h * half, 128), half)
        return jnp.concatenate(
            [dot(hidden, down[:, cols]), dot(preact_grad, up[cols, :], NT)], axis=0)

    def first_pass(src):
        hidden, preact_grad = expert(d, src)
        part[src] = columns_of(hidden, preact_grad, sib).astype(bf)
        p_copy(src).start()
        mine[src] = columns_of(hidden, preact_grad, c)

    def finish(src):
        p_copy(src).wait_recv()
        return (mine[src] + got[src].astype(jnp.float32)).astype(bf)

    first_pass(z)
    if n_ep == 4:
        z_copy(peer(2), z).wait_send()
        z_copy(peer(3), z).start()

    def block(i):
        src, last = peer(i), peer(i - 1)
        z_arrival(src).wait_recv()
        s_copy(d, src).start()
        for j in range(1, n_dp):
            x_copy(lax.rem(d + j, n_dp), src).start()
        if isinstance(i, int):
            if i == 1:
                back[z] = finish(z)
            else:
                ret[last] = finish(last)
                r_copy(last).start()
        else:
            ret[last] = finish(last)

            @pl.when(i == 1)
            def _():
                back[z] = ret[z]

            @pl.when(i > 1)
            def _():
                r_copy(last).start()
        s_arrival(d, src).wait_recv()
        first_pass(src)

    each((1, 2, 3), block)
    end = peer(n_ep - 1)
    ret[end] = finish(end)
    r_copy(end).start()

    def pass_on(t, _):
        frm, src = lax.rem(d + 1 + t // n_ep, n_dp), lax.rem(z + t, n_ep)
        x_arrival(frm, src).wait_recv()
        s_copy(frm, src).start()
        return 0

    lax.fori_loop(0, (n_dp - 1) * n_ep, pass_on, 0)

    def replica(t, _):
        frm, src = lax.rem(d + 1 + t // n_ep, n_dp), lax.rem(z + t, n_ep)
        s_arrival(frm, src).wait_recv()
        expert(frm, src)
        return 0

    lax.fori_loop(0, (n_dp - 1) * n_ep, replica, 0)

    share = width // n_dp
    at = d * share

    def gradients(group):
        if share == half:
            held = recv[group, d]
        else:
            held = recv[group, at // half, :, :, pl.ds(
                pl.multiple_of(lax.rem(at, half), 128), share)]
        held = held.reshape(n_ep * rows, share)
        inner = b_up.shape[-1]
        grad_up = dot(held, b_up[group].reshape(n_ep * rows, inner), TN)
        grad_down = dot(b_dn[group].reshape(n_ep * rows, inner), held, TN)
        return grad_up.astype(bf).astype(jnp.float32), grad_down.astype(bf).astype(jnp.float32)

    gu[...], gd[...] = gradients(0)

    def add_group(group, _):
        grad_up, grad_down = gradients(group)
        gu[...] += grad_up
        gd[...] += grad_down
        return 0

    lax.fori_loop(1, n_dp, add_group, 0)
    store_up = pltpu.make_async_copy(gu, gu_ref, o_sem.at[0])
    store_down = pltpu.make_async_copy(gd, gd_ref, o_sem.at[1])
    store_up.start()
    store_down.start()

    acc[...] = dot(route[z], back[z], TN)

    def collect(i):
        exp = peer(i)
        r_arrival(exp).wait_recv()
        acc[...] += dot(route[exp], back[exp], TN)

    each((1, 2, 3), collect)
    out_ref[...] = acc[:tok].astype(bf)
    in_ref[...] = acc[tok:].astype(bf)

    def drain(i):
        if n_ep != 4 or i != 2:
            z_copy(peer(i), z).wait_send()
        s_copy(d, peer(i)).wait_send()
        r_copy(peer(i)).wait_send()

    each((1, 2, 3), drain)

    def drain_all(t, _):
        p_copy(t).wait_send()
        for j in range(1, n_dp):
            x_copy(lax.rem(d + j, n_dp), t).wait_send()
            s_copy(lax.rem(d + j, n_dp), t).wait_send()
        return 0

    lax.fori_loop(0, n_ep, drain_all, 0)

    store_up.wait()
    store_down.wait()


def write_out(*refs):
    n = (len(refs) - 2) // 3
    sources, results, held = refs[:n], refs[n:2 * n], refs[2 * n:3 * n]
    in_sem, out_sem = refs[3 * n:]
    loads, stores = [], []
    for i in range(n):
        size = sources[i].shape[0]
        step = 128 if size % 128 == 0 else size
        for at in range(0, size, step):
            part, j = pl.ds(at, step), len(loads)
            loads.append(pltpu.make_async_copy(
                sources[i].at[part], held[i].at[part], in_sem.at[j]))
            stores.append(pltpu.make_async_copy(
                held[i].at[part], results[i].at[part], out_sem.at[j]))
    for load in loads:
        load.start()
    for load, store in zip(loads, stores):
        load.wait()
        store.start()
    for store in stores:
        store.wait()


def body(mesh, latent_in, out_grad, expert_ids, gate_weights, up_weight, down_weight):
    n_ep, n_dp = mesh.shape["ep"], mesh.shape["dp"]
    tok, width = latent_in.shape
    inner = up_weight.shape[2]
    assert up_weight.shape[0] == 1 and mesh.shape["tp"] == 2
    cap = 9 * tok * expert_ids.shape[1] // (8 * n_ep)
    cap = -(-cap // 8) * 8
    rows, half, share = 2 * cap, width // 2, width // n_dp
    bf, f32 = jnp.bfloat16, jnp.float32
    vmem = pl.BlockSpec(memory_space=pltpu.VMEM)
    hbm = pl.BlockSpec(memory_space=pltpu.HBM)
    dma = pltpu.SemaphoreType.DMA
    block = (n_ep, rows, half)
    results = (
        jax.ShapeDtypeStruct((share, inner), f32),
        jax.ShapeDtypeStruct((inner, share), f32),
        jax.ShapeDtypeStruct((tok, half), bf),
        jax.ShapeDtypeStruct((tok, half), bf),
    )
    held = pl.pallas_call(
        functools.partial(kernel, n_ep, n_dp, cap),
        out_shape=results,
        in_specs=[hbm] * 6,
        out_specs=(hbm, hbm, vmem, vmem),
        scratch_shapes=[
            pltpu.VMEM((tok, width), bf),
            pltpu.VMEM((tok, width), bf),
            pltpu.VMEM(expert_ids.shape[::-1], jnp.int32),
            pltpu.VMEM(gate_weights.shape[::-1], bf),
            pltpu.VMEM((width, inner), bf),
            pltpu.VMEM((inner, width), bf),
            pltpu.VMEM(block, bf),
            pltpu.VMEM((n_dp, 2) + block, bf),
            pltpu.VMEM((n_dp, n_ep, rows, inner), bf),
            pltpu.VMEM((n_dp, n_ep, rows, inner), bf),
            pltpu.VMEM(block, bf),
            pltpu.VMEM(block, bf),
            pltpu.VMEM(block, f32),
            pltpu.VMEM(block, bf),
            pltpu.VMEM(block, bf),
            pltpu.VMEM((n_ep, rows, 2 * tok), bf),
            pltpu.VMEM((2 * tok, half), f32),
            pltpu.VMEM((share, inner), f32),
            pltpu.VMEM((inner, share), f32),
            dma((6,)), dma((n_ep,)), dma((n_ep,)), dma((n_dp, n_ep)), dma((n_dp, n_ep)),
            dma((n_dp, n_ep)), dma((n_dp, n_ep)), dma((n_ep,)), dma((n_ep,)),
            dma((n_ep,)), dma((n_ep,)), dma((2,)),
        ],
        compiler_params=pltpu.CompilerParams(
            collective_id=0, has_side_effects=True, vmem_limit_bytes=58 * 1024 * 1024),
        name="routed_experts",
    )(latent_in, out_grad, expert_ids.T, gate_weights.T, up_weight, down_weight)
    count = sum(-(-r.shape[0] // 128) for r in results)
    grad_up, grad_down, out, lin = pl.pallas_call(
        write_out,
        out_shape=results,
        in_specs=[hbm] * 4,
        out_specs=(hbm,) * 4,
        scratch_shapes=[pltpu.VMEM(r.shape, r.dtype) for r in results] + [dma((count,))] * 2,
        compiler_params=pltpu.CompilerParams(vmem_limit_bytes=58 * 1024 * 1024),
        name="write_out",
    )(*held)
    return out, lin, grad_up[None], grad_down[None]


def solution(mesh):
    return jax.shard_map(
        functools.partial(body, mesh),
        mesh=mesh,
        in_specs=(
            P(("parts", "ep", "dp"), None),
            P(("parts", "ep", "dp"), None),
            P(("parts", "ep", "dp"), None),
            P(("parts", "ep", "dp"), None),
            P("ep", None, "tp"),
            P("ep", "tp", None),
        ),
        out_specs=(
            P(("parts", "ep", "dp"), "tp"),
            P(("parts", "ep", "dp"), "tp"),
            P(("parts", "ep"), "dp", "tp"),
            P(("parts", "ep"), "tp", "dp"),
        ),
        check_vma=False,
    )
```

```python
import functools

import jax
import jax.numpy as jnp
from jax import lax
from jax.experimental import pallas as pl
from jax.experimental.pallas import tpu as pltpu
from jax.sharding import PartitionSpec as P

MESH = pl.DeviceIdType.MESH
NT = (((1,), (1,)), ((), ()))
TN = (((0,), (0,)), ((), ()))


def dot(a, b, dims=(((1,), (0,)), ((), ()))):
    return lax.dot_general(a, b, dims, preferred_element_type=jnp.float32)


def kernel(
    n_ep, n_dp, cap,
    x_hbm, g_hbm, ids_hbm, gate_hbm, up_hbm, down_hbm,
    gu_ref, gd_ref, out_ref, in_ref,
    x_ref, g_ref, ids_ref, gate_ref, up, down, disp, recv, b_up, b_dn, part, got, mine, ret, back, route, acc, gu, gd,
    w_sem, z_send, z_recv, s_send, s_recv, x_send, x_recv, p_send, p_recv, r_send, r_recv, o_sem,
):
    z, d, c = lax.axis_index("ep"), lax.axis_index("dp"), lax.axis_index("tp")
    sib = 1 - c
    rows = 2 * cap
    tok, width = x_ref.shape
    half = width // 2
    fanout = ids_ref.shape[0]
    bf = jnp.bfloat16

    def peer(i):
        if n_ep == 4 and isinstance(i, int):
            return (z, z + 1 - 2 * lax.rem(z, 2), lax.rem(z + 2, 4), 3 - z)[i]
        return lax.rem(z + i, n_ep)

    def each(order, body):
        if n_ep == 4:
            for i in order:
                body(i)
        else:
            lax.fori_loop(1, n_ep, lambda i, _: (body(i), 0)[1], 0)

    load_x = pltpu.make_async_copy(x_hbm, x_ref, w_sem.at[0])
    load_g = pltpu.make_async_copy(g_hbm, g_ref, w_sem.at[1])
    load_up = pltpu.make_async_copy(up_hbm.at[0], up, w_sem.at[2])
    load_down = pltpu.make_async_copy(down_hbm.at[0], down, w_sem.at[3])
    load_ids = pltpu.make_async_copy(ids_hbm, ids_ref, w_sem.at[4])
    load_gate = pltpu.make_async_copy(gate_hbm, gate_ref, w_sem.at[5])
    load_ids.start()
    load_gate.start()
    load_x.start()
    load_g.start()
    barrier = pltpu.get_barrier_semaphore()

    def greet(i, _):
        pl.semaphore_signal(
            barrier, inc=1, device_id={"ep": lax.rem(z + i, n_ep)}, device_id_type=MESH)
        return 0

    lax.fori_loop(1, n_ep, greet, 0)
    for j in range(1, n_dp):
        pl.semaphore_signal(
            barrier, inc=1, device_id={"dp": lax.rem(d + j, n_dp)}, device_id_type=MESH)
    pl.semaphore_signal(barrier, inc=1, device_id={"tp": sib}, device_id_type=MESH)

    load_up.start()
    load_down.start()

    load_ids.wait()
    load_gate.wait()
    ids = ids_ref[...]
    height = -(-n_ep // 16) * 16
    numbers = lax.broadcasted_iota(jnp.int32, (height, tok), 0)
    picks = [(numbers == ids[k:k + 1, :]).astype(jnp.float32) for k in range(fanout)]
    named = functools.reduce(lambda a, b: a + b, picks).astype(bf)
    earlier = (
        lax.broadcasted_iota(jnp.int32, (tok, tok), 0)
        < lax.broadcasted_iota(jnp.int32, (tok, tok), 1)
    ).astype(jnp.float32).astype(bf)
    before = dot(named, earlier)
    gate = gate_ref[...].astype(jnp.float32)
    targets = [
        ids[k:k + 1, :].astype(jnp.float32) * float(rows)
        + jnp.sum(picks[k] * before, axis=0, keepdims=True)
        for k in range(fanout)]
    row = lax.broadcasted_iota(jnp.int32, (rows, tok), 0)

    def hits(exp, shift, weighted):
        slots = (row + (exp * rows - shift)).astype(jnp.float32)
        found = [
            jnp.where(slots == targets[k], gate[k:k + 1, :] if weighted else 1.0, 0.0)
            for k in range(fanout)]
        return functools.reduce(lambda a, b: a + b, found)

    def columns(h):
        return pl.ds(pl.multiple_of(h * half, 128), half)

    def build(exp, h):
        spread = jnp.concatenate(
            [hits(exp, 0, False), hits(exp, cap, True)], axis=1).astype(bf)
        source = jnp.concatenate([x_ref[:, columns(h)], g_ref[:, columns(h)]], axis=0)
        return dot(spread, source).astype(bf)

    load_x.wait()
    load_g.wait()

    def z_copy(dst, src):
        return pltpu.make_async_remote_copy(
            src_ref=disp.at[dst], dst_ref=recv.at[d, c, src],
            send_sem=z_send.at[dst], recv_sem=z_recv.at[src],
            device_id={"ep": dst}, device_id_type=MESH)

    def z_arrival(src):
        return pltpu.make_async_remote_copy(
            src_ref=disp.at[src], dst_ref=recv.at[d, c, src],
            send_sem=z_send.at[src], recv_sem=z_recv.at[src],
            device_id={"ep": src}, device_id_type=MESH)

    def x_copy(to, src):
        return pltpu.make_async_remote_copy(
            src_ref=recv.at[d, c, src], dst_ref=recv.at[d, c, src],
            send_sem=x_send.at[to, src], recv_sem=x_recv.at[d, src],
            device_id={"dp": to}, device_id_type=MESH)

    def x_arrival(frm, src):
        return pltpu.make_async_remote_copy(
            src_ref=recv.at[frm, c, src], dst_ref=recv.at[frm, c, src],
            send_sem=x_send.at[frm, src], recv_sem=x_recv.at[frm, src],
            device_id={"dp": frm}, device_id_type=MESH)

    def s_copy(group, src):
        return pltpu.make_async_remote_copy(
            src_ref=recv.at[group, c, src], dst_ref=recv.at[group, c, src],
            send_sem=s_send.at[group, src], recv_sem=s_recv.at[group, src],
            device_id={"tp": sib}, device_id_type=MESH)

    def s_arrival(group, src):
        return pltpu.make_async_remote_copy(
            src_ref=recv.at[group, sib, src], dst_ref=recv.at[group, sib, src],
            send_sem=s_send.at[group, src], recv_sem=s_recv.at[group, src],
            device_id={"tp": sib}, device_id_type=MESH)

    def p_copy(src):
        return pltpu.make_async_remote_copy(
            src_ref=part.at[src], dst_ref=got.at[src],
            send_sem=p_send.at[src], recv_sem=p_recv.at[src],
            device_id={"tp": sib}, device_id_type=MESH)

    def r_copy(src):
        return pltpu.make_async_remote_copy(
            src_ref=ret.at[src], dst_ref=back.at[z],
            send_sem=r_send.at[src], recv_sem=r_recv.at[z],
            device_id={"ep": src}, device_id_type=MESH)

    def r_arrival(exp):
        return pltpu.make_async_remote_copy(
            src_ref=ret.at[exp], dst_ref=back.at[exp],
            send_sem=r_send.at[exp], recv_sem=r_recv.at[exp],
            device_id={"ep": exp}, device_id_type=MESH)

    def send(i):
        dst = peer(i)
        disp[dst] = build(dst, c)
        z_copy(dst, z).start()

    if n_ep == 4:
        disp[peer(2)] = build(peer(2), c)
        pl.semaphore_wait(barrier, n_ep + n_dp - 1)
        z_copy(peer(2), z).start()
        send(1)
        disp[peer(3)] = build(peer(3), c)
    else:
        pl.semaphore_wait(barrier, n_ep + n_dp - 1)
        each((), send)

    recv[d, c, z] = build(z, c)
    recv[d, sib, z] = build(z, sib)
    for j in range(1, n_dp):
        x_copy(lax.rem(d + j, n_dp), z).start()

    def weigh(exp, _):
        route[exp] = jnp.concatenate(
            [hits(exp, 0, True), hits(exp, cap, False)], axis=1).astype(bf)
        return 0

    lax.fori_loop(0, n_ep, weigh, 0)
    load_up.wait()
    load_down.wait()

    def expert(group, src):
        left, right = recv[group, 0, src], recv[group, 1, src]
        left, right = left.astype(jnp.float32), right.astype(jnp.float32)
        r0, r1 = left[:cap].astype(bf), right[:cap].astype(bf)
        g0, g1 = left[cap:].astype(bf), right[cap:].astype(bf)
        preact = dot(r0, up[:half, :]) + dot(r1, up[half:, :])
        hidden_grad = dot(g0, down[:, :half], NT) + dot(g1, down[:, half:], NT)
        positive = jnp.maximum(preact, 0.0)
        hidden = positive * positive
        preact_grad = 2.0 * hidden_grad * positive
        nought = jnp.zeros_like(hidden)
        b_up[group, src] = jnp.concatenate([preact_grad, nought], axis=0).astype(bf)
        b_dn[group, src] = jnp.concatenate([nought, hidden], axis=0).astype(bf)
        return hidden.astype(bf), preact_grad.astype(bf)

    def columns_of(hidden, preact_grad, h):
        cols = pl.ds(pl.multiple_of(h * half, 128), half)
        return jnp.concatenate(
            [dot(hidden, down[:, cols]), dot(preact_grad, up[cols, :], NT)], axis=0)

    def first_pass(src):
        hidden, preact_grad = expert(d, src)
        part[src] = columns_of(hidden, preact_grad, sib).astype(bf)
        p_copy(src).start()
        mine[src] = columns_of(hidden, preact_grad, c)

    def finish(src):
        p_copy(src).wait_recv()
        return (mine[src] + got[src].astype(jnp.float32)).astype(bf)

    if n_ep == 4:
        z_copy(peer(2), z).wait_send()
        z_copy(peer(3), z).start()
    first_pass(z)

    def block(i):
        src, last = peer(i), peer(i - 1)
        if isinstance(i, int):
            if i > 1:
                ret[last] = finish(last)
                r_copy(last).start()
        else:
            ret[last] = finish(last)

            @pl.when(i == 1)
            def _():
                back[z] = ret[z]

            @pl.when(i > 1)
            def _():
                r_copy(last).start()
        z_arrival(src).wait_recv()
        s_copy(d, src).start()
        for j in range(1, n_dp):
            x_copy(lax.rem(d + j, n_dp), src).start()
        if isinstance(i, int) and i == 1:
            back[z] = finish(z)
        s_arrival(d, src).wait_recv()
        first_pass(src)

    each((1, 2, 3), block)
    end = peer(n_ep - 1)
    ret[end] = finish(end)
    r_copy(end).start()

    def pass_on(t, _):
        frm, src = lax.rem(d + 1 + t // n_ep, n_dp), lax.rem(z + t, n_ep)
        x_arrival(frm, src).wait_recv()
        s_copy(frm, src).start()
        return 0

    lax.fori_loop(0, (n_dp - 1) * n_ep, pass_on, 0)

    def replica(t, _):
        frm, src = lax.rem(d + 1 + t // n_ep, n_dp), lax.rem(z + t, n_ep)
        s_arrival(frm, src).wait_recv()
        expert(frm, src)
        return 0

    lax.fori_loop(0, (n_dp - 1) * n_ep, replica, 0)

    share = width // n_dp
    at = d * share

    def gradients(group):
        if share == half:
            held = recv[group, d]
        else:
            held = recv[group, at // half, :, :, pl.ds(
                pl.multiple_of(lax.rem(at, half), 128), share)]
        held = held.reshape(n_ep * rows, share)
        inner = b_up.shape[-1]
        grad_up = dot(held, b_up[group].reshape(n_ep * rows, inner), TN)
        grad_down = dot(b_dn[group].reshape(n_ep * rows, inner), held, TN)
        return grad_up.astype(bf).astype(jnp.float32), grad_down.astype(bf).astype(jnp.float32)

    gu[...], gd[...] = gradients(0)

    def add_group(group, _):
        grad_up, grad_down = gradients(group)
        gu[...] += grad_up
        gd[...] += grad_down
        return 0

    lax.fori_loop(1, n_dp, add_group, 0)
    store_up = pltpu.make_async_copy(gu, gu_ref, o_sem.at[0])
    store_down = pltpu.make_async_copy(gd, gd_ref, o_sem.at[1])
    store_up.start()
    store_down.start()

    acc[...] = dot(route[z], back[z], TN)

    def collect(i):
        exp = peer(i)
        r_arrival(exp).wait_recv()
        acc[...] += dot(route[exp], back[exp], TN)

    each((1, 2, 3), collect)
    out_ref[...] = acc[:tok].astype(bf)
    in_ref[...] = acc[tok:].astype(bf)

    def drain(i):
        if n_ep != 4 or i != 2:
            z_copy(peer(i), z).wait_send()
        s_copy(d, peer(i)).wait_send()
        r_copy(peer(i)).wait_send()

    each((1, 2, 3), drain)

    def drain_all(t, _):
        p_copy(t).wait_send()
        for j in range(1, n_dp):
            x_copy(lax.rem(d + j, n_dp), t).wait_send()
            s_copy(lax.rem(d + j, n_dp), t).wait_send()
        return 0

    lax.fori_loop(0, n_ep, drain_all, 0)

    store_up.wait()
    store_down.wait()


def write_out(*refs):
    n = (len(refs) - 2) // 3
    sources, results, held = refs[:n], refs[n:2 * n], refs[2 * n:3 * n]
    in_sem, out_sem = refs[3 * n:]
    loads, stores = [], []
    for i in range(n):
        size = sources[i].shape[0]
        step = 128 if size % 128 == 0 else size
        for at in range(0, size, step):
            part, j = pl.ds(at, step), len(loads)
            loads.append(pltpu.make_async_copy(
                sources[i].at[part], held[i].at[part], in_sem.at[j]))
            stores.append(pltpu.make_async_copy(
                held[i].at[part], results[i].at[part], out_sem.at[j]))
    for load in loads:
        load.start()
    for load, store in zip(loads, stores):
        load.wait()
        store.start()
    for store in stores:
        store.wait()


def body(mesh, latent_in, out_grad, expert_ids, gate_weights, up_weight, down_weight):
    n_ep, n_dp = mesh.shape["ep"], mesh.shape["dp"]
    tok, width = latent_in.shape
    inner = up_weight.shape[2]
    assert up_weight.shape[0] == 1 and mesh.shape["tp"] == 2
    cap = 9 * tok * expert_ids.shape[1] // (8 * n_ep)
    cap = -(-cap // 8) * 8
    rows, half, share = 2 * cap, width // 2, width // n_dp
    bf, f32 = jnp.bfloat16, jnp.float32
    vmem = pl.BlockSpec(memory_space=pltpu.VMEM)
    hbm = pl.BlockSpec(memory_space=pltpu.HBM)
    dma = pltpu.SemaphoreType.DMA
    block = (n_ep, rows, half)
    results = (
        jax.ShapeDtypeStruct((share, inner), f32),
        jax.ShapeDtypeStruct((inner, share), f32),
        jax.ShapeDtypeStruct((tok, half), bf),
        jax.ShapeDtypeStruct((tok, half), bf),
    )
    held = pl.pallas_call(
        functools.partial(kernel, n_ep, n_dp, cap),
        out_shape=results,
        in_specs=[hbm] * 6,
        out_specs=(hbm, hbm, vmem, vmem),
        scratch_shapes=[
            pltpu.VMEM((tok, width), bf),
            pltpu.VMEM((tok, width), bf),
            pltpu.VMEM(expert_ids.shape[::-1], jnp.int32),
            pltpu.VMEM(gate_weights.shape[::-1], bf),
            pltpu.VMEM((width, inner), bf),
            pltpu.VMEM((inner, width), bf),
            pltpu.VMEM(block, bf),
            pltpu.VMEM((n_dp, 2) + block, bf),
            pltpu.VMEM((n_dp, n_ep, rows, inner), bf),
            pltpu.VMEM((n_dp, n_ep, rows, inner), bf),
            pltpu.VMEM(block, bf),
            pltpu.VMEM(block, bf),
            pltpu.VMEM(block, f32),
            pltpu.VMEM(block, bf),
            pltpu.VMEM(block, bf),
            pltpu.VMEM((n_ep, rows, 2 * tok), bf),
            pltpu.VMEM((2 * tok, half), f32),
            pltpu.VMEM((share, inner), f32),
            pltpu.VMEM((inner, share), f32),
            dma((6,)), dma((n_ep,)), dma((n_ep,)), dma((n_dp, n_ep)), dma((n_dp, n_ep)),
            dma((n_dp, n_ep)), dma((n_dp, n_ep)), dma((n_ep,)), dma((n_ep,)),
            dma((n_ep,)), dma((n_ep,)), dma((2,)),
        ],
        compiler_params=pltpu.CompilerParams(
            collective_id=0, has_side_effects=True, vmem_limit_bytes=58 * 1024 * 1024),
        name="routed_experts",
    )(latent_in, out_grad, expert_ids.T, gate_weights.T, up_weight, down_weight)
    count = sum(-(-r.shape[0] // 128) for r in results)
    grad_up, grad_down, out, lin = pl.pallas_call(
        write_out,
        out_shape=results,
        in_specs=[hbm] * 4,
        out_specs=(hbm,) * 4,
        scratch_shapes=[pltpu.VMEM(r.shape, r.dtype) for r in results] + [dma((count,))] * 2,
        compiler_params=pltpu.CompilerParams(vmem_limit_bytes=58 * 1024 * 1024),
        name="write_out",
    )(*held)
    return out, lin, grad_up[None], grad_down[None]


def solution(mesh):
    return jax.shard_map(
        functools.partial(body, mesh),
        mesh=mesh,
        in_specs=(
            P(("parts", "ep", "dp"), None),
            P(("parts", "ep", "dp"), None),
            P(("parts", "ep", "dp"), None),
            P(("parts", "ep", "dp"), None),
            P("ep", None, "tp"),
            P("ep", "tp", None),
        ),
        out_specs=(
            P(("parts", "ep", "dp"), "tp"),
            P(("parts", "ep", "dp"), "tp"),
            P(("parts", "ep"), "dp", "tp"),
            P(("parts", "ep"), "tp", "dp"),
        ),
        check_vma=False,
    )
```

```python
import functools

import jax
import jax.numpy as jnp
from jax import lax
from jax.experimental import pallas as pl
from jax.experimental.pallas import tpu as pltpu
from jax.sharding import PartitionSpec as P

MESH = pl.DeviceIdType.MESH
NT = (((1,), (1,)), ((), ()))
TN = (((0,), (0,)), ((), ()))


def dot(a, b, dims=(((1,), (0,)), ((), ()))):
    return lax.dot_general(a, b, dims, preferred_element_type=jnp.float32)


def kernel(
    n_ep, n_dp, cap,
    x_hbm, g_hbm, ids_hbm, gate_hbm, up_hbm, down_hbm,
    gu_ref, gd_ref, out_ref, in_ref,
    x_ref, g_ref, ids_ref, gate_ref, up, down, disp, recv, b_up, b_dn, part, got, mine, ret, back, route, acc, gu, gd,
    w_sem, z_send, z_recv, s_send, s_recv, x_send, x_recv, p_send, p_recv, r_send, r_recv, o_sem,
):
    z, d, c = lax.axis_index("ep"), lax.axis_index("dp"), lax.axis_index("tp")
    sib = 1 - c
    rows = 2 * cap
    tok, width = x_ref.shape
    half = width // 2
    fanout = ids_ref.shape[0]
    bf = jnp.bfloat16

    def peer(i):
        if n_ep == 4 and isinstance(i, int):
            return (z, z + 1 - 2 * lax.rem(z, 2), lax.rem(z + 2, 4), 3 - z)[i]
        return lax.rem(z + i, n_ep)

    def each(order, body):
        if n_ep == 4:
            for i in order:
                body(i)
        else:
            lax.fori_loop(1, n_ep, lambda i, _: (body(i), 0)[1], 0)

    load_x = pltpu.make_async_copy(x_hbm, x_ref, w_sem.at[0])
    load_g = pltpu.make_async_copy(g_hbm, g_ref, w_sem.at[1])
    load_up = pltpu.make_async_copy(up_hbm.at[0], up, w_sem.at[2])
    load_down = pltpu.make_async_copy(down_hbm.at[0], down, w_sem.at[3])
    load_ids = pltpu.make_async_copy(ids_hbm, ids_ref, w_sem.at[4])
    load_gate = pltpu.make_async_copy(gate_hbm, gate_ref, w_sem.at[5])
    load_ids.start()
    load_gate.start()
    load_x.start()
    load_g.start()
    barrier = pltpu.get_barrier_semaphore()

    def greet(i, _):
        pl.semaphore_signal(
            barrier, inc=1, device_id={"ep": lax.rem(z + i, n_ep)}, device_id_type=MESH)
        return 0

    lax.fori_loop(1, n_ep, greet, 0)
    for j in range(1, n_dp):
        pl.semaphore_signal(
            barrier, inc=1, device_id={"dp": lax.rem(d + j, n_dp)}, device_id_type=MESH)
    pl.semaphore_signal(barrier, inc=1, device_id={"tp": sib}, device_id_type=MESH)


    load_ids.wait()
    load_gate.wait()
    ids = ids_ref[...]
    height = -(-n_ep // 16) * 16
    numbers = lax.broadcasted_iota(jnp.int32, (height, tok), 0)
    picks = [(numbers == ids[k:k + 1, :]).astype(jnp.float32) for k in range(fanout)]
    named = functools.reduce(lambda a, b: a + b, picks).astype(bf)
    earlier = (
        lax.broadcasted_iota(jnp.int32, (tok, tok), 0)
        < lax.broadcasted_iota(jnp.int32, (tok, tok), 1)
    ).astype(jnp.float32).astype(bf)
    before = dot(named, earlier)
    gate = gate_ref[...].astype(jnp.float32)
    targets = [
        ids[k:k + 1, :].astype(jnp.float32) * float(rows)
        + jnp.sum(picks[k] * before, axis=0, keepdims=True)
        for k in range(fanout)]
    row = lax.broadcasted_iota(jnp.int32, (rows, tok), 0)

    def hits(exp, shift, weighted):
        slots = (row + (exp * rows - shift)).astype(jnp.float32)
        found = [
            jnp.where(slots == targets[k], gate[k:k + 1, :] if weighted else 1.0, 0.0)
            for k in range(fanout)]
        return functools.reduce(lambda a, b: a + b, found)

    def columns(h):
        return pl.ds(pl.multiple_of(h * half, 128), half)

    def build(exp, h):
        spread = jnp.concatenate(
            [hits(exp, 0, False), hits(exp, cap, True)], axis=1).astype(bf)
        source = jnp.concatenate([x_ref[:, columns(h)], g_ref[:, columns(h)]], axis=0)
        return dot(spread, source).astype(bf)

    load_x.wait()
    load_g.wait()
    load_up.start()
    load_down.start()

    def z_copy(dst, src):
        return pltpu.make_async_remote_copy(
            src_ref=disp.at[dst], dst_ref=recv.at[d, c, src],
            send_sem=z_send.at[dst], recv_sem=z_recv.at[src],
            device_id={"ep": dst}, device_id_type=MESH)

    def z_arrival(src):
        return pltpu.make_async_remote_copy(
            src_ref=disp.at[src], dst_ref=recv.at[d, c, src],
            send_sem=z_send.at[src], recv_sem=z_recv.at[src],
            device_id={"ep": src}, device_id_type=MESH)

    def x_copy(to, src):
        return pltpu.make_async_remote_copy(
            src_ref=recv.at[d, c, src], dst_ref=recv.at[d, c, src],
            send_sem=x_send.at[to, src], recv_sem=x_recv.at[d, src],
            device_id={"dp": to}, device_id_type=MESH)

    def x_arrival(frm, src):
        return pltpu.make_async_remote_copy(
            src_ref=recv.at[frm, c, src], dst_ref=recv.at[frm, c, src],
            send_sem=x_send.at[frm, src], recv_sem=x_recv.at[frm, src],
            device_id={"dp": frm}, device_id_type=MESH)

    def s_copy(group, src):
        return pltpu.make_async_remote_copy(
            src_ref=recv.at[group, c, src], dst_ref=recv.at[group, c, src],
            send_sem=s_send.at[group, src], recv_sem=s_recv.at[group, src],
            device_id={"tp": sib}, device_id_type=MESH)

    def s_arrival(group, src):
        return pltpu.make_async_remote_copy(
            src_ref=recv.at[group, sib, src], dst_ref=recv.at[group, sib, src],
            send_sem=s_send.at[group, src], recv_sem=s_recv.at[group, src],
            device_id={"tp": sib}, device_id_type=MESH)

    def p_copy(src):
        return pltpu.make_async_remote_copy(
            src_ref=part.at[src], dst_ref=got.at[src],
            send_sem=p_send.at[src], recv_sem=p_recv.at[src],
            device_id={"tp": sib}, device_id_type=MESH)

    def r_copy(src):
        return pltpu.make_async_remote_copy(
            src_ref=ret.at[src], dst_ref=back.at[z],
            send_sem=r_send.at[src], recv_sem=r_recv.at[z],
            device_id={"ep": src}, device_id_type=MESH)

    def r_arrival(exp):
        return pltpu.make_async_remote_copy(
            src_ref=ret.at[exp], dst_ref=back.at[exp],
            send_sem=r_send.at[exp], recv_sem=r_recv.at[exp],
            device_id={"ep": exp}, device_id_type=MESH)

    def send(i):
        dst = peer(i)
        disp[dst] = build(dst, c)
        z_copy(dst, z).start()

    if n_ep == 4:
        disp[peer(2)] = build(peer(2), c)
        pl.semaphore_wait(barrier, n_ep + n_dp - 1)
        z_copy(peer(2), z).start()
        send(1)
        disp[peer(3)] = build(peer(3), c)
    else:
        pl.semaphore_wait(barrier, n_ep + n_dp - 1)
        each((), send)

    recv[d, c, z] = build(z, c)
    recv[d, sib, z] = build(z, sib)
    for j in range(1, n_dp):
        x_copy(lax.rem(d + j, n_dp), z).start()

    def weigh(exp, _):
        route[exp] = jnp.concatenate(
            [hits(exp, 0, True), hits(exp, cap, False)], axis=1).astype(bf)
        return 0

    lax.fori_loop(0, n_ep, weigh, 0)
    load_up.wait()
    load_down.wait()

    def expert(group, src):
        left, right = recv[group, 0, src], recv[group, 1, src]
        left, right = left.astype(jnp.float32), right.astype(jnp.float32)
        r0, r1 = left[:cap].astype(bf), right[:cap].astype(bf)
        g0, g1 = left[cap:].astype(bf), right[cap:].astype(bf)
        preact = dot(r0, up[:half, :]) + dot(r1, up[half:, :])
        hidden_grad = dot(g0, down[:, :half], NT) + dot(g1, down[:, half:], NT)
        positive = jnp.maximum(preact, 0.0)
        hidden = positive * positive
        preact_grad = 2.0 * hidden_grad * positive
        nought = jnp.zeros_like(hidden)
        b_up[group, src] = jnp.concatenate([preact_grad, nought], axis=0).astype(bf)
        b_dn[group, src] = jnp.concatenate([nought, hidden], axis=0).astype(bf)
        return hidden.astype(bf), preact_grad.astype(bf)

    def columns_of(hidden, preact_grad, h):
        cols = pl.ds(pl.multiple_of(h * half, 128), half)
        return jnp.concatenate(
            [dot(hidden, down[:, cols]), dot(preact_grad, up[cols, :], NT)], axis=0)

    def first_pass(src):
        hidden, preact_grad = expert(d, src)
        part[src] = columns_of(hidden, preact_grad, sib).astype(bf)
        p_copy(src).start()
        mine[src] = columns_of(hidden, preact_grad, c)

    def finish(src):
        p_copy(src).wait_recv()
        return (mine[src] + got[src].astype(jnp.float32)).astype(bf)

    if n_ep == 4:
        z_copy(peer(2), z).wait_send()
        z_copy(peer(3), z).start()
    first_pass(z)

    def block(i):
        src, last = peer(i), peer(i - 1)
        if isinstance(i, int):
            if i > 1:
                ret[last] = finish(last)
                r_copy(last).start()
        else:
            ret[last] = finish(last)

            @pl.when(i == 1)
            def _():
                back[z] = ret[z]

            @pl.when(i > 1)
            def _():
                r_copy(last).start()
        z_arrival(src).wait_recv()
        s_copy(d, src).start()
        for j in range(1, n_dp):
            x_copy(lax.rem(d + j, n_dp), src).start()
        if isinstance(i, int) and i == 1:
            back[z] = finish(z)
        s_arrival(d, src).wait_recv()
        first_pass(src)

    each((1, 2, 3), block)
    end = peer(n_ep - 1)
    ret[end] = finish(end)
    r_copy(end).start()

    def pass_on(t, _):
        frm, src = lax.rem(d + 1 + t // n_ep, n_dp), lax.rem(z + t, n_ep)
        x_arrival(frm, src).wait_recv()
        s_copy(frm, src).start()
        return 0

    lax.fori_loop(0, (n_dp - 1) * n_ep, pass_on, 0)

    def replica(t, _):
        frm, src = lax.rem(d + 1 + t // n_ep, n_dp), lax.rem(z + t, n_ep)
        s_arrival(frm, src).wait_recv()
        expert(frm, src)
        return 0

    lax.fori_loop(0, (n_dp - 1) * n_ep, replica, 0)

    share = width // n_dp
    at = d * share

    def gradients(group):
        if share == half:
            held = recv[group, d]
        else:
            held = recv[group, at // half, :, :, pl.ds(
                pl.multiple_of(lax.rem(at, half), 128), share)]
        held = held.reshape(n_ep * rows, share)
        inner = b_up.shape[-1]
        grad_up = dot(held, b_up[group].reshape(n_ep * rows, inner), TN)
        grad_down = dot(b_dn[group].reshape(n_ep * rows, inner), held, TN)
        return grad_up.astype(bf).astype(jnp.float32), grad_down.astype(bf).astype(jnp.float32)

    gu[...], gd[...] = gradients(0)

    def add_group(group, _):
        grad_up, grad_down = gradients(group)
        gu[...] += grad_up
        gd[...] += grad_down
        return 0

    lax.fori_loop(1, n_dp, add_group, 0)
    store_up = pltpu.make_async_copy(gu, gu_ref, o_sem.at[0])
    store_down = pltpu.make_async_copy(gd, gd_ref, o_sem.at[1])
    store_up.start()
    store_down.start()

    acc[...] = dot(route[z], back[z], TN)

    def collect(i):
        exp = peer(i)
        r_arrival(exp).wait_recv()
        acc[...] += dot(route[exp], back[exp], TN)

    each((1, 2, 3), collect)
    out_ref[...] = acc[:tok].astype(bf)
    in_ref[...] = acc[tok:].astype(bf)

    def drain(i):
        if n_ep != 4 or i != 2:
            z_copy(peer(i), z).wait_send()
        s_copy(d, peer(i)).wait_send()
        r_copy(peer(i)).wait_send()

    each((1, 2, 3), drain)

    def drain_all(t, _):
        p_copy(t).wait_send()
        for j in range(1, n_dp):
            x_copy(lax.rem(d + j, n_dp), t).wait_send()
            s_copy(lax.rem(d + j, n_dp), t).wait_send()
        return 0

    lax.fori_loop(0, n_ep, drain_all, 0)

    store_up.wait()
    store_down.wait()


def write_out(*refs):
    n = (len(refs) - 2) // 3
    sources, results, held = refs[:n], refs[n:2 * n], refs[2 * n:3 * n]
    in_sem, out_sem = refs[3 * n:]
    loads, stores = [], []
    for i in range(n):
        size = sources[i].shape[0]
        step = 256 if size % 256 == 0 else size
        for at in range(0, size, step):
            part, j = pl.ds(at, step), len(loads)
            loads.append(pltpu.make_async_copy(
                sources[i].at[part], held[i].at[part], in_sem.at[j]))
            stores.append(pltpu.make_async_copy(
                held[i].at[part], results[i].at[part], out_sem.at[j]))
    for load in loads:
        load.start()
    for load, store in zip(loads, stores):
        load.wait()
        store.start()
    for store in stores:
        store.wait()


def body(mesh, latent_in, out_grad, expert_ids, gate_weights, up_weight, down_weight):
    n_ep, n_dp = mesh.shape["ep"], mesh.shape["dp"]
    tok, width = latent_in.shape
    inner = up_weight.shape[2]
    assert up_weight.shape[0] == 1 and mesh.shape["tp"] == 2
    cap = 9 * tok * expert_ids.shape[1] // (8 * n_ep)
    cap = -(-cap // 8) * 8
    rows, half, share = 2 * cap, width // 2, width // n_dp
    bf, f32 = jnp.bfloat16, jnp.float32
    vmem = pl.BlockSpec(memory_space=pltpu.VMEM)
    hbm = pl.BlockSpec(memory_space=pltpu.HBM)
    dma = pltpu.SemaphoreType.DMA
    block = (n_ep, rows, half)
    results = (
        jax.ShapeDtypeStruct((share, inner), f32),
        jax.ShapeDtypeStruct((inner, share), f32),
        jax.ShapeDtypeStruct((tok, half), bf),
        jax.ShapeDtypeStruct((tok, half), bf),
    )
    held = pl.pallas_call(
        functools.partial(kernel, n_ep, n_dp, cap),
        out_shape=results,
        in_specs=[hbm] * 6,
        out_specs=(hbm, hbm, vmem, vmem),
        scratch_shapes=[
            pltpu.VMEM((tok, width), bf),
            pltpu.VMEM((tok, width), bf),
            pltpu.VMEM(expert_ids.shape[::-1], jnp.int32),
            pltpu.VMEM(gate_weights.shape[::-1], bf),
            pltpu.VMEM((width, inner), bf),
            pltpu.VMEM((inner, width), bf),
            pltpu.VMEM(block, bf),
            pltpu.VMEM((n_dp, 2) + block, bf),
            pltpu.VMEM((n_dp, n_ep, rows, inner), bf),
            pltpu.VMEM((n_dp, n_ep, rows, inner), bf),
            pltpu.VMEM(block, bf),
            pltpu.VMEM(block, bf),
            pltpu.VMEM(block, f32),
            pltpu.VMEM(block, bf),
            pltpu.VMEM(block, bf),
            pltpu.VMEM((n_ep, rows, 2 * tok), bf),
            pltpu.VMEM((2 * tok, half), f32),
            pltpu.VMEM((share, inner), f32),
            pltpu.VMEM((inner, share), f32),
            dma((6,)), dma((n_ep,)), dma((n_ep,)), dma((n_dp, n_ep)), dma((n_dp, n_ep)),
            dma((n_dp, n_ep)), dma((n_dp, n_ep)), dma((n_ep,)), dma((n_ep,)),
            dma((n_ep,)), dma((n_ep,)), dma((2,)),
        ],
        compiler_params=pltpu.CompilerParams(
            collective_id=0, has_side_effects=True, vmem_limit_bytes=58 * 1024 * 1024),
        name="routed_experts",
    )(latent_in, out_grad, expert_ids.T, gate_weights.T, up_weight, down_weight)
    count = sum(-(-r.shape[0] // 256) for r in results)
    grad_up, grad_down, out, lin = pl.pallas_call(
        write_out,
        out_shape=results,
        in_specs=[hbm] * 4,
        out_specs=(hbm,) * 4,
        scratch_shapes=[pltpu.VMEM(r.shape, r.dtype) for r in results] + [dma((count,))] * 2,
        compiler_params=pltpu.CompilerParams(vmem_limit_bytes=58 * 1024 * 1024),
        name="write_out",
    )(*held)
    return out, lin, grad_up[None], grad_down[None]


def solution(mesh):
    return jax.shard_map(
        functools.partial(body, mesh),
        mesh=mesh,
        in_specs=(
            P(("parts", "ep", "dp"), None),
            P(("parts", "ep", "dp"), None),
            P(("parts", "ep", "dp"), None),
            P(("parts", "ep", "dp"), None),
            P("ep", None, "tp"),
            P("ep", "tp", None),
        ),
        out_specs=(
            P(("parts", "ep", "dp"), "tp"),
            P(("parts", "ep", "dp"), "tp"),
            P(("parts", "ep"), "dp", "tp"),
            P(("parts", "ep"), "tp", "dp"),
        ),
        check_vma=False,
    )
```
